32 devices in a mesh: dp: 8 (over z, core), mp: 4 (over y, x).
Axes of the slice: x: 2, y: 2, z: 4, core: 2. Of those that a mesh axis runs over, the one named last changes fastest.
Arguments:
- grads: bfloat16 [8192, 2048], P('mp', 'dp'), may hold values from -24 to 24
- old_factor: float32 [8192, 8192], P('mp', 'dp'), may hold values from -1 to 16, as said below
- basis: float32 [8192, 512], P('mp', 'dp'), may hold values from -6 to 6
Outputs:
- new_factor: float32 [8192, 8192], P('mp', 'dp')
- new_basis: float32 [8192, 512], P('mp', 'dp')
- basis_one: float32 [8192, 512], P('dp')
The draws below stay inside these ranges and needn't reach their ends.
Inputs may be any that keep to these rules, and one draw needn't show every extreme that they name: old_factor is symmetric; its diagonal lies between 1 and 16 and its off-diagonal entries between -2.3/sqrt(8192) and 2.3/sqrt(8192).
All inputs are finite; a program needn't handle non-finite values.
Results may differ from the reference program's by a relative error of at most 0.0003.
Values may be sent and summed in bfloat16 or wider, within the bound.
A program may use at most 256 MiB of HBM per device.

```python
import math
import jax
import jax.numpy as jnp
from jax import lax

D = 8192
F = 2048
K = 512


def draw_old_factor(key, part):
    key = jax.random.fold_in(key, 7)
    noise_key, diag_key = jax.random.split(key)
    position = lax.broadcasted_iota(jnp.int32, (D,), 0).astype(jnp.float32) / D
    noise = jnp.clip(jax.random.normal(noise_key, (D, D), jnp.float32), -4.0, 4.0)
    rough = jax.random.uniform(diag_key, (D,), jnp.float32, 0.0, math.log(3.0))
    diag = jnp.exp(rough + math.log(10.0 / 3.0) * position)
    symmetric = (noise + noise.T) * (0.70710678 * 0.4 / math.sqrt(D))
    rows = lax.broadcasted_iota(jnp.int32, (D, D), 0)
    cols = lax.broadcasted_iota(jnp.int32, (D, D), 1)
    return jnp.where(rows == cols, diag[:, None], symmetric)


def shard_levels(rng, shape, cuts, low, top_value):
    gain, own = 1.0, jax.random.fold_in(rng, 6)
    for axis_at, blocks in cuts:
        draws = jnp.exp(jax.random.uniform(jax.random.fold_in(own, axis_at), (blocks,), jnp.float32, low / len(cuts), top_value / len(cuts)))
        gain = gain * jnp.repeat(draws, shape[axis_at] // blocks).reshape([-1 if axis == axis_at else 1 for axis in range(len(shape))])
    return gain


def bell_draw(own_key, dims, deviation, most, cuts=(), dtype=jnp.bfloat16):
    result = jax.random.normal(own_key, dims, jnp.float32) * deviation
    if len(cuts) > 0:
        result = shard_levels(own_key, dims, cuts, -0.22, 0.18) * result
    return jnp.clip(result, min=-most, max=most).astype(dtype)


def setup_inputs(seed: int = 0) -> dict:
    key_list = jax.random.split(jax.random.key(seed), 4)
    return {
        "grads": bell_draw(key_list[0], (D, F), 4.0, 24.0, ((0, 4), (1, 8))),
        "old_factor": draw_old_factor(jax.random.fold_in(key_list[3], 71), 0),
        "basis": bell_draw(key_list[2], (D, K), 1.0, 6.0, ((0, 4), (1, 8)), jnp.float32),
    }


def orthonormal(product):
    high = lax.Precision.HIGHEST
    gram = jnp.dot(product.T.astype(jnp.float32), product.astype(jnp.float32), precision=high, preferred_element_type=jnp.float32) / D
    lower = jnp.linalg.cholesky(gram)
    solved = lax.linalg.triangular_solve(lower, product.T, left_side=True, lower=True)
    return solved.T

def reference(grads, old_factor, basis):
    high = lax.Precision.HIGHEST
    widened = grads.astype(jnp.float32)
    summed = jnp.dot(widened.astype(jnp.float32), widened.T.astype(jnp.float32), precision=high, preferred_element_type=jnp.float32)
    new_factor = 0.95 * old_factor + 0.05 / F * summed
    product_one = jnp.dot(new_factor.astype(jnp.float32), basis.astype(jnp.float32), precision=high, preferred_element_type=jnp.float32)
    basis_one = orthonormal(product_one)
    product_two = jnp.dot(new_factor.astype(jnp.float32), basis_one.astype(jnp.float32), precision=high, preferred_element_type=jnp.float32)
    new_basis = orthonormal(product_two)
    return (new_factor, new_basis, basis_one)
```

```python
import functools

import jax
import jax.numpy as jnp
from jax import lax
from jax.experimental import pallas as pl
from jax.experimental.pallas import tpu as pltpu
from jax.sharding import PartitionSpec as P

D = 8192
MESH = pl.DeviceIdType.MESH
HIGHEST = lax.Precision.HIGHEST
BLOCK = 128
STEP = 8


def dot(left, right, dims, precision=HIGHEST):
    return lax.dot_general(
        left, right, (dims, ((), ())), precision=precision, preferred_element_type=jnp.float32
    )


def invert_block(block, step):
    n = block.shape[0]
    row_id = lax.broadcasted_iota(jnp.int32, (n, n), 0)
    col_id = lax.broadcasted_iota(jnp.int32, (n, n), 1)
    left = block
    right = jnp.where(row_id == col_id, 1.0, 0.0).astype(jnp.float32)
    done = []
    for k in range(0, n, step):
        low = k // 8 * 8
        if low + left.shape[0] > n:
            cut = low - (n - left.shape[0])
            done.append((right[:cut], pivots))
            left, right = left[cut:], right[cut:]
        if k % 8 == 0:
            pivots = jnp.zeros((8, n), jnp.float32)
        ids = row_id[low:]
        reps = [jnp.broadcast_to(left[:, k + p : k + p + 1], left.shape) for p in range(step)]
        for p in range(step):
            at = k + p - low
            pivots = jnp.where(row_id[:8] == at, reps[p][:8], pivots)
            inverse = 1.0 / reps[p][at : at + 1]
            mult = jnp.where(ids > k + p, reps[p] * inverse, 0.0)
            for q in range(p + 1, step):
                reps[q] = reps[q] - mult * reps[q][at : at + 1]
            left = left - mult * left[at : at + 1]
            right = right - mult * right[at : at + 1]
    done.append((right, pivots))
    return jnp.concatenate([r * lax.rsqrt(p) for r, p in done], axis=0)


def factor_kernel(gram_ref, out_ref, work):
    n = gram_ref.shape[0]
    work[...] = gram_ref[...]
    row_id = lax.broadcasted_iota(jnp.int32, (n, n), 0)
    col_id = lax.broadcasted_iota(jnp.int32, (n, n), 1)
    out_ref[...] = jnp.where(row_id == col_id, 1.0, 0.0).astype(jnp.float32)

    def body(b, carry):
        at = pl.multiple_of(b * BLOCK, BLOCK)
        inv = invert_block(work[pl.ds(at, BLOCK), pl.ds(at, BLOCK)], STEP)
        upper = dot(inv, work[pl.ds(at, BLOCK), :], ((1,), (0,)))
        side = dot(inv, out_ref[pl.ds(at, BLOCK), :], ((1,), (0,)))
        keep = lax.broadcasted_iota(jnp.int32, (BLOCK, n), 1) >= at + BLOCK
        below = jnp.where(keep, upper, 0.0)
        work[...] -= dot(below, upper, ((0,), (0,)))
        out_ref[...] -= dot(below, side, ((0,), (0,)))
        out_ref[pl.ds(at, BLOCK), :] = side
        return carry

    lax.fori_loop(0, n // BLOCK, body, 0)


def inverse_factor(gram):
    return pl.pallas_call(
        factor_kernel,
        out_shape=jax.ShapeDtypeStruct(gram.shape, jnp.float32),
        in_specs=[pl.BlockSpec(memory_space=pltpu.VMEM)],
        out_specs=pl.BlockSpec(memory_space=pltpu.VMEM),
        scratch_shapes=[pltpu.VMEM(gram.shape, jnp.float32)],
        compiler_params=pltpu.CompilerParams(vmem_limit_bytes=40 * 2**20),
    )(gram)


def rows_at(index, size):
    return pl.ds(pl.multiple_of(index * size, size), size)


def place():
    dp, mp = lax.axis_index("dp"), lax.axis_index("mp")
    return dp, mp, dp // 2, lax.rem(dp, 2)


def partners(num_mp, num_z):
    dp, mp, z, core = place()
    pair = (z * 2 + 1 - core, mp)
    across = [lax.rem(mp + d, num_mp) for d in range(1, num_mp)]
    along = [lax.rem(z + d, num_z) for d in range(1, num_z)]
    return pair, [((dp, p), p) for p in across], [((p * 2 + core, mp), p) for p in along]


def meet(targets):
    barrier = pltpu.get_barrier_semaphore()
    for target in targets:
        pl.semaphore_signal(barrier, inc=1, device_id=target, device_id_type=MESH)
    pl.semaphore_wait(barrier, len(targets))


def sender(send_sem, recv_sem):
    count = [0]

    def send(source, landing, target):
        at = count[0]
        count[0] += 1
        copy = pltpu.make_async_remote_copy(
            src_ref=source,
            dst_ref=landing,
            send_sem=send_sem.at[at],
            recv_sem=recv_sem.at[at],
            device_id=target,
            device_id_type=MESH,
        )
        copy.start()
        return copy

    return send


def finish(copies):
    for copy in copies:
        copy.wait()


def total(slots):
    result = slots[0]
    for index in range(1, slots.shape[0]):
        result = result + slots[index]
    return result


def sum_gram(send, groups, part, pair_box, half, mp_box, z_box, full):
    pair, across, along = groups
    _, mp, z, core = place()
    half_rows, rows = half.shape[0], mp_box.shape[1]
    finish([send(part.at[rows_at(1 - core, half_rows)], pair_box, pair)])
    half[...] = part[rows_at(core, half_rows), :] + pair_box[...]
    copies = [send(half.at[rows_at(p, rows)], mp_box.at[mp], to) for to, p in across]
    mp_box[mp] = half[rows_at(mp, rows), :]
    finish(copies)
    z_box[z] = total(mp_box) * (1.0 / D)
    finish([send(z_box.at[z], z_box.at[z], to) for to, _ in along])
    own = rows_at(core * (half_rows // rows) + mp, rows)
    full[own, :] = total(z_box)
    finish([send(full.at[own], full.at[own], to) for to, _ in across])
    mine = rows_at(core, half_rows)
    finish([send(full.at[mine], full.at[mine], pair)])


def gram_scratch(n, num_mp, num_z):
    rows = n // 2 // num_mp
    shapes = [(n, n), (n // 2, n), (n // 2, n), (num_mp, rows, n), (num_z, rows, n), (n, n)]
    return [pltpu.VMEM(shape, jnp.float32) for shape in shapes]


def first_kernel(num_mp, num_z, part_ref, gram_ref, sum_ref, box, whole, *rest):
    *work, send_sem, recv_sem = rest
    groups = partners(num_mp, num_z)
    pair, across, along = groups
    _, mp, _, _ = place()
    send = sender(send_sem, recv_sem)
    chunk = box.shape[1]
    meet([pair] + [to for to, _ in across + along])
    copies = [send(part_ref.at[rows_at(p, chunk)], box.at[mp], to) for to, p in across]
    box[mp] = part_ref[rows_at(mp, chunk), :]
    finish(copies)
    own = rows_at(mp, chunk)
    mine = total(box)
    whole[own, :] = mine
    spread = [send(whole.at[own], whole.at[own], to) for to, _ in across]
    work[0][...] = dot(mine, mine, ((0,), (0,)))
    sum_gram(send, groups, *work)
    gram_ref[...] = work[-1][...]
    finish(spread)
    sum_ref[...] = whole[...]


def second_kernel(num_mp, num_z, part_ref, gram_ref, sum_ref, pair_sum, joined, box, *rest):
    *work, send_sem, recv_sem = rest
    groups = partners(num_mp, num_z)
    pair, across, along = groups
    _, _, z, core = place()
    send = sender(send_sem, recv_sem)
    half_rows, chunk = joined.shape[0], box.shape[1]
    meet([pair] + [to for to, _ in across + along])
    finish([send(part_ref.at[rows_at(1 - core, half_rows)], pair_sum, pair)])
    joined[...] = part_ref[rows_at(core, half_rows), :] + pair_sum[...]
    copies = [send(joined.at[rows_at(p, chunk)], box.at[z], to) for to, p in along]
    box[z] = joined[rows_at(z, chunk), :]
    finish(copies)
    mine = total(box)
    sum_ref[...] = mine
    work[0][...] = dot(mine, mine, ((0,), (0,)))
    sum_gram(send, groups, *work)
    gram_ref[...] = work[-1][...]


def swap_kernel(num_dp, part_ref, out_ref, box, send_sem, recv_sem):
    dp, mp, _, _ = place()
    width = box.shape[1]
    others = [lax.rem(dp + d, num_dp) for d in range(1, num_dp)]
    send = sender(send_sem, recv_sem)
    meet([(p, mp) for p in others])
    copies = [send(part_ref.at[rows_at(p, width)], box.at[dp], (p, mp)) for p in others]
    box[dp] = part_ref[rows_at(dp, width), :]
    finish(copies)
    out_ref[...] = box[...]


def remote_call(body, collective_id, outs, scratch, copies, value):
    vmem = pl.BlockSpec(memory_space=pltpu.VMEM)
    return pl.pallas_call(
        body,
        out_shape=[jax.ShapeDtypeStruct(shape, jnp.float32) for shape in outs],
        in_specs=[vmem],
        out_specs=[vmem] * len(outs),
        scratch_shapes=scratch
        + [pltpu.SemaphoreType.DMA((copies,)), pltpu.SemaphoreType.DMA((copies,))],
        compiler_params=pltpu.CompilerParams(
            collective_id=collective_id, has_side_effects=True, vmem_limit_bytes=48 * 2**20
        ),
    )(value)


def sum_first(part, num_mp, num_z):
    height, n = part.shape
    chunk = height // num_mp
    scratch = [
        pltpu.VMEM((num_mp, chunk, n), jnp.float32),
        pltpu.VMEM((height, n), jnp.float32),
    ] + gram_scratch(n, num_mp, num_z)
    copies = 4 * (num_mp - 1) + num_z - 1 + 2
    body = functools.partial(first_kernel, num_mp, num_z)
    return remote_call(body, 0, [(n, n), (height, n)], scratch, copies, part)


def sum_second(part, num_mp, num_z):
    height, n = part.shape
    chunk = height // 2 // num_z
    scratch = [
        pltpu.VMEM((height // 2, n), jnp.float32),
        pltpu.VMEM((height // 2, n), jnp.float32),
        pltpu.VMEM((num_z, chunk, n), jnp.float32),
    ] + gram_scratch(n, num_mp, num_z)
    copies = 2 * (num_mp - 1) + 2 * (num_z - 1) + 3
    body = functools.partial(second_kernel, num_mp, num_z)
    return remote_call(body, 1, [(n, n), (chunk, n)], scratch, copies, part)


def swap(part, num_dp):
    n, chunk = part.shape
    shape = (num_dp, n // num_dp, chunk)
    scratch = [pltpu.VMEM(shape, jnp.float32)]
    return remote_call(
        functools.partial(swap_kernel, num_dp), 2, [shape], scratch, num_dp - 1, part
    )[0]


def from_root(value, axis, root):
    mine = lax.axis_index(axis) == root
    return lax.psum(jnp.where(mine, value, jnp.zeros_like(value)), axis)


def body(grads, old_factor, basis):
    cols_here = old_factor.shape[1]
    num_mp = lax.axis_size("mp")
    num_dp = lax.axis_size("dp")
    num_z = num_dp // 2
    total_cols = grads.shape[1] * num_dp
    high = lax.Precision.HIGH
    basis_full = lax.all_gather(basis, "dp", axis=1, tiled=True)
    stripe_full = lax.all_gather(grads, "dp", axis=1, tiled=True)
    ratio = num_dp // num_mp
    offset = lax.axis_index("dp") % ratio * cols_here
    local_panel = lax.dynamic_slice_in_dim(stripe_full, offset, cols_here, 0)
    panel_full = from_root(local_panel, "mp", lax.axis_index("dp") // ratio)
    summed_block = lax.dot_general(
        stripe_full, panel_full, (((1,), (1,)), ((), ())), preferred_element_type=jnp.float32
    )
    new_factor = 0.95 * old_factor + 0.05 / total_cols * summed_block
    part_one = dot(new_factor, basis_full, ((0,), (0,)), high)
    gram_one, product_one = sum_first(part_one, num_mp, num_z)
    basis_one = dot(product_one, inverse_factor(gram_one), ((1,), (1,)))
    part_two = dot(new_factor, basis_one, ((1,), (0,)), high)
    gram_two, product_two = sum_second(part_two, num_mp, num_z)
    basis_two = dot(inverse_factor(gram_two), product_two, ((1,), (1,)))
    blocks = swap(basis_two, num_dp)
    blocks = blocks.reshape(num_z, 2, *blocks.shape[1:])
    new_basis = blocks.transpose(1, 0, 3, 2).reshape(basis.shape)
    return (new_factor, new_basis, basis_one)


def solution(mesh):
    placed = (P("mp", "dp"), P("mp", "dp"), P("mp", "dp"))
    return jax.shard_map(
        body,
        mesh=mesh,
        in_specs=placed,
        out_specs=(P("mp", "dp"), P("mp", "dp"), P("dp", None)),
        check_vma=False,
    )
```

```python
import functools

import jax
import jax.numpy as jnp
from jax import lax
from jax.experimental import pallas as pl
from jax.experimental.pallas import tpu as pltpu
from jax.sharding import PartitionSpec as P

D = 8192
MESH = pl.DeviceIdType.MESH
HIGHEST = lax.Precision.HIGHEST
BLOCK = 128
STEP = 8


def dot(left, right, dims, precision=HIGHEST):
    return lax.dot_general(
        left, right, (dims, ((), ())), precision=precision, preferred_element_type=jnp.float32
    )


def invert_block(block, step):
    n = block.shape[0]
    row_id = lax.broadcasted_iota(jnp.int32, (n, n), 0)
    col_id = lax.broadcasted_iota(jnp.int32, (n, n), 1)
    left = block
    right = jnp.where(row_id == col_id, 1.0, 0.0).astype(jnp.float32)
    done = []
    for k in range(0, n, step):
        low = k // 8 * 8
        if low + left.shape[0] > n:
            cut = low - (n - left.shape[0])
            done.append((right[:cut], pivots))
            left, right = left[cut:], right[cut:]
        if k % 8 == 0:
            pivots = jnp.zeros((8, n), jnp.float32)
        ids = row_id[low:]
        reps = [jnp.broadcast_to(left[:, k + p : k + p + 1], left.shape) for p in range(step)]
        for p in range(step):
            at = k + p - low
            pivots = jnp.where(row_id[:8] == at, reps[p][:8], pivots)
            inverse = 1.0 / reps[p][at : at + 1]
            mult = jnp.where(ids > k + p, reps[p] * inverse, 0.0)
            for q in range(p + 1, step):
                reps[q] = reps[q] - mult * reps[q][at : at + 1]
            left = left - mult * left[at : at + 1]
            right = right - mult * right[at : at + 1]
    done.append((right, pivots))
    return jnp.concatenate([r * lax.rsqrt(p) for r, p in done], axis=0)


def factor_kernel(gram_ref, out_ref, work):
    n = gram_ref.shape[0]
    work[...] = gram_ref[...]
    row_id = lax.broadcasted_iota(jnp.int32, (n, n), 0)
    col_id = lax.broadcasted_iota(jnp.int32, (n, n), 1)
    out_ref[...] = jnp.where(row_id == col_id, 1.0, 0.0).astype(jnp.float32)

    def body(b, carry):
        at = pl.multiple_of(b * BLOCK, BLOCK)
        inv = invert_block(work[pl.ds(at, BLOCK), pl.ds(at, BLOCK)], STEP)
        upper = dot(inv, work[pl.ds(at, BLOCK), :], ((1,), (0,)))
        side = dot(inv, out_ref[pl.ds(at, BLOCK), :], ((1,), (0,)))
        keep = lax.broadcasted_iota(jnp.int32, (BLOCK, n), 1) >= at + BLOCK
        below = jnp.where(keep, upper, 0.0)
        work[...] -= dot(below, upper, ((0,), (0,)))
        out_ref[...] -= dot(below, side, ((0,), (0,)))
        out_ref[pl.ds(at, BLOCK), :] = side
        return carry

    lax.fori_loop(0, n // BLOCK, body, 0)


def inverse_factor(gram):
    return pl.pallas_call(
        factor_kernel,
        out_shape=jax.ShapeDtypeStruct(gram.shape, jnp.float32),
        in_specs=[pl.BlockSpec(memory_space=pltpu.VMEM)],
        out_specs=pl.BlockSpec(memory_space=pltpu.VMEM),
        scratch_shapes=[pltpu.VMEM(gram.shape, jnp.float32)],
        compiler_params=pltpu.CompilerParams(vmem_limit_bytes=40 * 2**20),
    )(gram)


def rows_at(index, size):
    return pl.ds(pl.multiple_of(index * size, size), size)


def place():
    dp, mp = lax.axis_index("dp"), lax.axis_index("mp")
    return dp, mp, dp // 2, lax.rem(dp, 2)


def partners(num_mp, num_z):
    dp, mp, z, core = place()
    pair = (z * 2 + 1 - core, mp)
    across = [lax.rem(mp + d, num_mp) for d in range(1, num_mp)]
    along = [lax.rem(z + d, num_z) for d in range(1, num_z)]
    return pair, [((dp, p), p) for p in across], [((p * 2 + core, mp), p) for p in along]


def meet(targets):
    barrier = pltpu.get_barrier_semaphore()
    for target in targets:
        pl.semaphore_signal(barrier, inc=1, device_id=target, device_id_type=MESH)
    pl.semaphore_wait(barrier, len(targets))


def sender(send_sem, recv_sem):
    count = [0]

    def send(source, landing, target):
        at = count[0]
        count[0] += 1
        copy = pltpu.make_async_remote_copy(
            src_ref=source,
            dst_ref=landing,
            send_sem=send_sem.at[at],
            recv_sem=recv_sem.at[at],
            device_id=target,
            device_id_type=MESH,
        )
        copy.start()
        return copy

    return send


def finish(copies):
    for copy in copies:
        copy.wait()


def total(slots):
    result = slots[0]
    for index in range(1, slots.shape[0]):
        result = result + slots[index]
    return result


def sum_gram(send, groups, part, pair_box, half, mp_box, z_box, full):
    pair, across, along = groups
    _, mp, z, core = place()
    half_rows, rows = half.shape[0], mp_box.shape[1]
    finish([send(part.at[rows_at(1 - core, half_rows)], pair_box, pair)])
    half[...] = part[rows_at(core, half_rows), :] + pair_box[...]
    copies = [send(half.at[rows_at(p, rows)], mp_box.at[mp], to) for to, p in across]
    mp_box[mp] = half[rows_at(mp, rows), :]
    finish(copies)
    z_box[z] = total(mp_box) * (1.0 / D)
    finish([send(z_box.at[z], z_box.at[z], to) for to, _ in along])
    own = rows_at(core * (half_rows // rows) + mp, rows)
    full[own, :] = total(z_box)
    finish([send(full.at[own], full.at[own], to) for to, _ in across])
    mine = rows_at(core, half_rows)
    finish([send(full.at[mine], full.at[mine], pair)])


def gram_scratch(n, num_mp, num_z):
    rows = n // 2 // num_mp
    shapes = [(n, n), (n // 2, n), (n // 2, n), (num_mp, rows, n), (num_z, rows, n), (n, n)]
    return [pltpu.VMEM(shape, jnp.float32) for shape in shapes]


def first_kernel(num_mp, num_z, part_ref, gram_ref, sum_ref, box, whole, *rest):
    *work, send_sem, recv_sem = rest
    groups = partners(num_mp, num_z)
    pair, across, along = groups
    _, mp, _, _ = place()
    send = sender(send_sem, recv_sem)
    chunk = box.shape[1]
    meet([pair] + [to for to, _ in across + along])
    copies = [send(part_ref.at[rows_at(p, chunk)], box.at[mp], to) for to, p in across]
    box[mp] = part_ref[rows_at(mp, chunk), :]
    finish(copies)
    own = rows_at(mp, chunk)
    mine = total(box)
    whole[own, :] = mine
    spread = [send(whole.at[own], whole.at[own], to) for to, _ in across]
    work[0][...] = dot(mine, mine, ((0,), (0,)))
    sum_gram(send, groups, *work)
    gram_ref[...] = work[-1][...]
    finish(spread)
    sum_ref[...] = whole[...]


def second_kernel(num_mp, num_z, part_ref, gram_ref, sum_ref, pair_sum, joined, box, *rest):
    *work, send_sem, recv_sem = rest
    groups = partners(num_mp, num_z)
    pair, across, along = groups
    _, _, z, core = place()
    send = sender(send_sem, recv_sem)
    half_rows, chunk = joined.shape[0], box.shape[1]
    meet([pair] + [to for to, _ in across + along])
    finish([send(part_ref.at[rows_at(1 - core, half_rows)], pair_sum, pair)])
    joined[...] = part_ref[rows_at(core, half_rows), :] + pair_sum[...]
    copies = [send(joined.at[rows_at(p, chunk)], box.at[z], to) for to, p in along]
    box[z] = joined[rows_at(z, chunk), :]
    finish(copies)
    mine = total(box)
    sum_ref[...] = mine
    work[0][...] = dot(mine, mine, ((0,), (0,)))
    sum_gram(send, groups, *work)
    gram_ref[...] = work[-1][...]


def swap_kernel(num_dp, part_ref, out_ref, box, send_sem, recv_sem):
    dp, mp, _, _ = place()
    width = box.shape[1]
    others = [lax.rem(dp + d, num_dp) for d in range(1, num_dp)]
    send = sender(send_sem, recv_sem)
    meet([(p, mp) for p in others])
    copies = [send(part_ref.at[rows_at(p, width)], box.at[dp], (p, mp)) for p in others]
    box[dp] = part_ref[rows_at(dp, width), :]
    finish(copies)
    out_ref[...] = box[...]


def remote_call(body, collective_id, outs, scratch, copies, value):
    vmem = pl.BlockSpec(memory_space=pltpu.VMEM)
    return pl.pallas_call(
        body,
        out_shape=[jax.ShapeDtypeStruct(shape, jnp.float32) for shape in outs],
        in_specs=[vmem],
        out_specs=[vmem] * len(outs),
        scratch_shapes=scratch
        + [pltpu.SemaphoreType.DMA((copies,)), pltpu.SemaphoreType.DMA((copies,))],
        compiler_params=pltpu.CompilerParams(
            collective_id=collective_id, has_side_effects=True, vmem_limit_bytes=48 * 2**20
        ),
    )(value)


def sum_first(part, num_mp, num_z):
    height, n = part.shape
    chunk = height // num_mp
    scratch = [
        pltpu.VMEM((num_mp, chunk, n), jnp.float32),
        pltpu.VMEM((height, n), jnp.float32),
    ] + gram_scratch(n, num_mp, num_z)
    copies = 4 * (num_mp - 1) + num_z - 1 + 2
    body = functools.partial(first_kernel, num_mp, num_z)
    return remote_call(body, 0, [(n, n), (height, n)], scratch, copies, part)


def sum_second(part, num_mp, num_z):
    height, n = part.shape
    chunk = height // 2 // num_z
    scratch = [
        pltpu.VMEM((height // 2, n), jnp.float32),
        pltpu.VMEM((height // 2, n), jnp.float32),
        pltpu.VMEM((num_z, chunk, n), jnp.float32),
    ] + gram_scratch(n, num_mp, num_z)
    copies = 2 * (num_mp - 1) + 2 * (num_z - 1) + 3
    body = functools.partial(second_kernel, num_mp, num_z)
    return remote_call(body, 1, [(n, n), (chunk, n)], scratch, copies, part)


def swap(part, num_dp):
    n, chunk = part.shape
    shape = (num_dp, n // num_dp, chunk)
    scratch = [pltpu.VMEM(shape, jnp.float32)]
    return remote_call(
        functools.partial(swap_kernel, num_dp), 2, [shape], scratch, num_dp - 1, part
    )[0]


CHUNKS = 8


def snake(index, side):
    row, col = index // side, lax.rem(index, side)
    return row * side + col + lax.rem(row, 2) * (side - 1 - 2 * col)


def panel_kernel(num_dp, num_mp, side, stripe_ref, out_ref, panel, local_sem, send_sem, recv_sem):
    dp, mp, _, _ = place()
    ratio = num_dp // num_mp
    height = panel.shape[0]
    chunk = height // 2 // CHUNKS
    at = snake(mp, side)
    root = snake(dp // ratio, side)
    after = (dp, snake(lax.rem(at + 1, num_mp), side))
    before = (dp, snake(lax.rem(at + num_mp - 1, num_mp), side))
    meet([after, before])
    ways = (
        (lax.rem(at - root + num_mp, num_mp), after),
        (lax.rem(root - at + num_mp, num_mp), before),
    )

    @pl.when(at == root)
    def _():
        mine = stripe_ref.at[rows_at(lax.rem(dp, ratio), height)]
        copy = pltpu.make_async_copy(mine, panel, local_sem)
        copy.start()
        copy.wait()

    def piece(way, step):
        rows = panel.at[pl.ds((way * CHUNKS + step) * chunk, chunk)]
        return pltpu.make_async_remote_copy(
            src_ref=rows,
            dst_ref=rows,
            send_sem=send_sem.at[way, step],
            recv_sem=recv_sem.at[way, step],
            device_id=ways[way][1],
            device_id_type=MESH,
        )

    for step in range(CHUNKS):
        for way in range(2):
            pl.when(ways[way][0] > 0)(piece(way, step).wait_recv)
            pl.when(ways[way][0] < num_mp - 1)(piece(way, step).start)
    for way in range(2):
        for step in range(CHUNKS):
            pl.when(ways[way][0] < num_mp - 1)(piece(way, step).wait_send)
    copy = pltpu.make_async_copy(panel, out_ref, local_sem)
    copy.start()
    copy.wait()


def gather_panel(stripe, cols_here, num_dp, num_mp):
    side = max(s for s in range(1, num_mp + 1) if s * s <= num_mp)
    shape = (cols_here, stripe.shape[1])
    return pl.pallas_call(
        functools.partial(panel_kernel, num_dp, num_mp, side),
        out_shape=jax.ShapeDtypeStruct(shape, stripe.dtype),
        in_specs=[pl.BlockSpec(memory_space=pl.ANY)],
        out_specs=pl.BlockSpec(memory_space=pl.ANY),
        scratch_shapes=[
            pltpu.VMEM(shape, stripe.dtype),
            pltpu.SemaphoreType.DMA,
            pltpu.SemaphoreType.DMA((2, CHUNKS)),
            pltpu.SemaphoreType.DMA((2, CHUNKS)),
        ],
        compiler_params=pltpu.CompilerParams(
            collective_id=3, has_side_effects=True, vmem_limit_bytes=48 * 2**20
        ),
        cost_estimate=pl.CostEstimate(flops=0, bytes_accessed=128 * 2**20, transcendentals=0),
    )(stripe)


def split(value):
    top = value.astype(jnp.bfloat16)
    return top, (value - top.astype(jnp.float32)).astype(jnp.bfloat16)


def factor_step(scale, old_ref, stripe_ref, panel_ref, basis_ref, new_ref, part_ref):
    height = old_ref.shape[0]
    tall = min(height, 512)
    inner = ((1,), (0,))
    result = jnp.zeros(part_ref.shape[::-1], jnp.float32)
    for start in range(0, height, tall):
        rows = pl.ds(start, tall)
        summed = dot(stripe_ref[rows, :], panel_ref[...], ((1,), (1,)), None)
        value = 0.95 * old_ref[rows, :] + scale * summed
        new_ref[rows, :] = value
        top, low = split(value)
        basis_top, basis_low = split(basis_ref[:, rows])
        result += dot(basis_top, top, inner, None)
        result += dot(basis_low, top, inner, None) + dot(basis_top, low, inner, None)
    part_ref[...] = result.T


def update_factor(old_factor, stripe, panel, basis_full):
    height, width = old_factor.shape
    depth, n = stripe.shape[1], basis_full.shape[0]
    tile = 256
    whole = lambda i: (0, 0)
    return pl.pallas_call(
        functools.partial(factor_step, 0.05 / depth),
        grid=(width // tile,),
        out_shape=[
            jax.ShapeDtypeStruct((height, width), jnp.float32),
            jax.ShapeDtypeStruct((width, n), jnp.float32),
        ],
        in_specs=[
            pl.BlockSpec((height, tile), lambda i: (0, i)),
            pl.BlockSpec((height, depth), whole, pipeline_mode=pl.Buffered(1)),
            pl.BlockSpec((tile, depth), lambda i: (i, 0)),
            pl.BlockSpec((n, height), whole, pipeline_mode=pl.Buffered(1)),
        ],
        out_specs=[
            pl.BlockSpec((height, tile), lambda i: (0, i)),
            pl.BlockSpec((tile, n), lambda i: (i, 0)),
        ],
        compiler_params=pltpu.CompilerParams(vmem_limit_bytes=48 * 2**20),
    )(old_factor, stripe, panel, basis_full)


def body(grads, old_factor, basis):
    cols_here = old_factor.shape[1]
    num_mp = lax.axis_size("mp")
    num_dp = lax.axis_size("dp")
    num_z = num_dp // 2
    high = lax.Precision.HIGH
    stripe_full = lax.all_gather(grads, "dp", axis=1, tiled=True)
    basis_rows, stripe_full = lax.optimization_barrier((basis.T, stripe_full))
    basis_full = lax.all_gather(basis_rows, "dp", axis=0, tiled=True)
    panel_full = gather_panel(stripe_full, cols_here, num_dp, num_mp)
    new_factor, part_one = update_factor(old_factor, stripe_full, panel_full, basis_full)
    gram_one, product_one = sum_first(part_one, num_mp, num_z)
    basis_one = dot(product_one, inverse_factor(gram_one), ((1,), (1,)))
    part_two = dot(new_factor, basis_one, ((1,), (0,)), high)
    gram_two, product_two = sum_second(part_two, num_mp, num_z)
    basis_two = dot(inverse_factor(gram_two), product_two, ((1,), (1,)))
    blocks = swap(basis_two, num_dp)
    blocks = blocks.reshape(num_z, 2, *blocks.shape[1:])
    new_basis = blocks.transpose(1, 0, 3, 2).reshape(basis.shape)
    return (new_factor, new_basis, basis_one)


def solution(mesh):
    placed = (P("mp", "dp"), P("mp", "dp"), P("mp", "dp"))
    return jax.shard_map(
        body,
        mesh=mesh,
        in_specs=placed,
        out_specs=(P("mp", "dp"), P("mp", "dp"), P("dp", None)),
        check_vma=False,
    )
```
